32 devices in a mesh: leaf: 8 (over z, x), rows: 4 (over y, core).
Axes of the slice: x: 2, y: 2, z: 4, core: 2. Of those that a mesh axis runs over, the one named last changes fastest.
Arguments:
- child_front_entries: float32 [8, 4, 4, 128, 2048], P('leaf', None, 'rows'), may hold values from 0 to 2, as said below
- parent_fronts: float32 [8, 4, 4, 128, 2048], P('leaf', None, 'rows'), may hold values from 0 to 2, as said below
- parent_of: int32 [8], replicated, may hold values from 0 to 3, never falling along the last dimension, each value on 1 to 4 neighbouring positions
- positions: int32 [8, 8], P('leaf'), may hold values from 0 to 15, as said below
Outputs:
- child_factor: float32 [8, 4, 4, 128, 1024], P('leaf', None, 'rows')
- parent_factor: float32 [8, 4, 4, 128, 1024], P('leaf', None, 'rows')
- parent_contribution_block: float32 [8, 2, 4, 128, 1024], P('leaf', None, 'rows')
The draws below stay inside these ranges and needn't reach their ends.
Inputs may be any that keep to these rules, and one draw needn't show every extreme that they name: `parent_of`: children of one parent stand at consecutive indices, at most 4 of them, and some parent has exactly 4; every parent has a child. `positions`: each row lists 8 distinct parent block numbers in increasing order; the last is always 16 - 1. `child_front_entries`: each front is symmetric positive definite. `parent_fronts`: each front is symmetric positive definite.
All inputs are finite; a program needn't handle non-finite values.
Results may differ from the reference program's by a relative error of at most 0.000078.
Values sent between devices are 32-bit elements; how exact they have to be, the bound alone decides.
A program may use at most 256 MiB of HBM per device.

```python
import math
import jax
import jax.numpy as jnp
import numpy as np
from jax import lax

F = 2048
B = 128
PIV = 1024
MOST = 4
CHILDREN = 8
PARENTS = 4
FB = 16
CBW = 1024
CB_BLK = 8
N_ROWS = 4


def kernel_front(sub_key):
    sub_keys = jax.random.split(sub_key, 3)
    box_side = 2.6
    centers = jax.random.uniform(sub_keys[0], (FB, 1, 3), jnp.float32, 0.0, box_side)
    jitter = jax.random.uniform(sub_keys[1], (FB, B, 3), jnp.float32, -0.3, 0.3)
    points = (centers + jitter).reshape(F, 3)
    diagonal_jitter_term = jax.random.uniform(sub_keys[2], (F,), jnp.float32, 0.3, 1.0)
    squared = jnp.zeros((F, F), jnp.float32)
    for coord_no in range(3):
        coord_gap = points[:, coord_no][:, None] - points[:, coord_no][None, :]
        squared = squared + coord_gap * coord_gap
    distance = jnp.sqrt(squared)
    closeness = jnp.maximum(1.0 - distance, 0.0)
    kernel_value = closeness ** 4 * (4.0 * distance + 1.0)
    return kernel_value + jnp.diag(diagonal_jitter_term)


def front_scales(base_key):
    phase = jax.random.uniform(jax.random.fold_in(base_key, 53), (), jnp.float32, 0.0, 6.2831853)
    front_index = jnp.arange(CHILDREN, dtype=jnp.float32)
    weight_level = 0.5 + 0.5 * jnp.sin(phase + 0.15 * front_index)
    return jnp.exp(-4.0 * 2.302585093 * weight_level)


def draw_fronts(front_key, base_key):
    sub_keys = jax.random.split(front_key, CHILDREN)
    fronts = lax.map(kernel_front, sub_keys)
    scales = front_scales(base_key)
    fronts = fronts * scales[:, None, None]
    return fronts.reshape(CHILDREN, FB // N_ROWS, N_ROWS, B, F)


def draw_child_front_entries(key, part):
    return draw_fronts(jax.random.fold_in(key, 11), key)


def draw_parent_fronts(key, part):
    return draw_fronts(jax.random.fold_in(key, 23), key)


def draw_positions(key, part):
    scores = jax.random.randint(jax.random.fold_in(key, 37), (CHILDREN, FB - 1), 0, 1 << 20) * FB + jnp.arange(FB - 1, dtype=jnp.int32)
    top_scores = lax.top_k(scores, CB_BLK - 1)[1]
    chosen = jnp.sort(top_scores.astype(jnp.int32), axis=-1)
    last_block = jnp.full((CHILDREN, 1), FB - 1, jnp.int32)
    return jnp.concatenate([chosen, last_block], axis=1)


def profile(amount, total, most, lean):
    loads = [(1 << 20) // math.isqrt(standing ** lean) + 1 for standing in range(2, amount + 1)]
    rest, holding = total - most - (amount - 1), [1] * (amount - 1)
    while rest > 0:
        candidates = [i for i in range(amount - 1) if holding[i] < most]
        whole, budget = sum([loads[i] for i in candidates]), rest
        for i in candidates:
            more = min(most - holding[i], max(1, budget * loads[i] // whole), rest)
            holding[i] = holding[i] + more
            rest = rest - more
    return np.array([most] + holding)


def ragged_sizes(own_key, number_of, total, bound, lean):
    if number_of == 2:
        one = jax.random.randint(own_key, (), max(1, total - bound), min(bound, total - 1) + 1)
        return jnp.stack([one, total - one])
    lengths = jnp.asarray(profile(number_of, total, bound, lean), jnp.int32)
    pairs = (number_of - 1) // 2
    giver, sink = lengths[1:1 + 2 * pairs:2], lengths[2:2 + 2 * pairs:2]
    room = jnp.minimum(giver - 1, bound - sink)
    shifted = jax.random.randint(jax.random.fold_in(own_key, 1), (pairs,), 0, 1 << 20) % (room + 1)
    lengths = lengths.at[1:1 + 2 * pairs:2].set(giver - shifted).at[2:2 + 2 * pairs:2].set(sink + shifted)
    return lengths[jax.random.permutation(jax.random.fold_in(own_key, 2), number_of)]


def setup_inputs(seed: int = 0) -> dict:
    arg_keys = jax.random.split(jax.random.key(seed), 5)
    child_front_entries = draw_child_front_entries(jax.random.fold_in(arg_keys[4], 71), 0)
    parent_fronts = draw_parent_fronts(jax.random.fold_in(arg_keys[4], 71), 0)
    parent_of = jnp.searchsorted(jnp.cumsum(ragged_sizes(arg_keys[2], PARENTS, CHILDREN, MOST, 2)), jnp.arange(CHILDREN), side="right").astype(jnp.int32)
    positions = draw_positions(jax.random.fold_in(arg_keys[4], 71), 0)
    return {"child_front_entries": child_front_entries, "parent_fronts": parent_fronts, "parent_of": parent_of, "positions": positions}


def factor_front(front_matrix):
    pivot_part = front_matrix[:PIV, :PIV]
    lower_factor = jnp.linalg.cholesky(pivot_part)
    below_factor = lax.linalg.triangular_solve(lower_factor, front_matrix[PIV:, :PIV], left_side=False, lower=True, transpose_a=True)
    factor_cols = jnp.concatenate([lower_factor, below_factor], axis=0)
    schur_part = front_matrix[PIV:, PIV:] - jnp.dot(below_factor, below_factor.T, precision=lax.Precision.HIGHEST)
    return (factor_cols, schur_part)

def reference(child_front_entries, parent_fronts, parent_of, positions):
    child_total = child_front_entries.shape[0]
    child_mats = child_front_entries.reshape(child_total, F, F)
    parent_mats = parent_fronts.reshape(child_total, F, F)
    child_cols, child_updates = lax.map(factor_front, child_mats)
    block_onehot = (positions[:, :, None] == jnp.arange(FB, dtype=jnp.int32)[None, None, :]).astype(jnp.float32)
    update_blocks = child_updates.reshape(child_total, CB_BLK, B, CB_BLK, B)
    extended = jnp.einsum('kap,kaibj,kbq->kpiqj', block_onehot, update_blocks, block_onehot, precision=lax.Precision.HIGHEST)
    extended = extended.reshape(child_total, F, F)
    previous = jnp.concatenate([jnp.full((1,), -1, jnp.int32), parent_of[:-1]])
    head_flags = parent_of != previous
    leaf_ids = jnp.arange(child_total, dtype=jnp.int32)
    head_of = lax.cummax(jnp.where(head_flags, leaf_ids, 0), axis=0).astype(jnp.int32)
    assembled = parent_mats.at[head_of].add(extended)
    parent_cols, parent_schur = lax.map(factor_front, assembled)
    head_mask = head_flags.astype(jnp.float32)[:, None, None]
    parent_cols = parent_cols * head_mask
    parent_schur = parent_schur * head_mask
    child_out = child_cols.reshape(child_total, FB // N_ROWS, N_ROWS, B, PIV)
    parent_out = parent_cols.reshape(child_total, FB // N_ROWS, N_ROWS, B, PIV)
    update_out = parent_schur.reshape(child_total, CB_BLK // N_ROWS, N_ROWS, B, CBW)
    return (child_out, parent_out, update_out)
```

```python
import functools

import jax
import jax.numpy as jnp
from jax import lax
from jax.experimental import pallas as pl
from jax.experimental.pallas import tpu as pltpu
from jax.sharding import PartitionSpec as P

B = 128
PIV = 1024
MOST = 4
SUB = 8
VMEM_LIMIT = 48 * 1024 * 1024


def from_behind(block, axis, distance):
    devices = range(lax.axis_size(axis))
    route = [(i - distance, i) for i in devices if i - distance in devices]
    return lax.ppermute(block, axis, route)


def dot_t(a, b):
    return lax.dot_general(
        a,
        b,
        (((1,), (1,)), ((), ())),
        precision=lax.Precision.HIGHEST,
        preferred_element_type=jnp.float32,
    )


def eliminate(block, upper_ref, inverse_ref):
    size = block.shape[0]
    groups = size // SUB
    lane = lax.broadcasted_iota(jnp.int32, (SUB, size), 1)
    sub = lax.broadcasted_iota(jnp.int32, (SUB, size), 0)
    left = [block[SUB * u : SUB * (u + 1), :] for u in range(groups)]
    right = [jnp.where(lane == sub + SUB * u, 1.0, 0.0) for u in range(groups)]
    sub_column = lax.broadcasted_iota(jnp.int32, (SUB, 1), 0)
    for j in range(size):
        t, s = divmod(j, SUB)
        row_left = left[t][s : s + 1, :]
        row_right = right[t][s : s + 1, :]
        pivot = row_left[:, j : j + 1]
        scale = lax.rsqrt(pivot)
        upper_ref[j : j + 1, :] = row_left * scale
        inverse_ref[j : j + 1, :] = row_right * scale
        over = 1.0 / pivot
        unit_left = row_left * over
        unit_right = row_right * over
        for u in range(t, groups):
            column = left[u][:, j : j + 1]
            if u == t:
                column = jnp.where(sub_column > s, column, 0.0)
            left[u] = left[u] - column * unit_left
            right[u] = right[u] - column * unit_right


def factor_kernel(pivot_ref, low_ref, out_ref, upper_ref, inverse_ref, *, chunk):
    width = pivot_ref.shape[0]
    total = out_ref.shape[0]
    panels = width // B
    chunks = total // chunk
    out_ref[:width, :] = pivot_ref[...]
    out_ref[width:, :] = low_ref[...]
    row = lax.broadcasted_iota(jnp.int32, (B, B), 0)
    col = lax.broadcasted_iota(jnp.int32, (B, B), 1)

    @pl.loop(0, panels)
    def _(k):
        first = pl.multiple_of(k * B, B)
        here = pl.ds(first, B)
        eliminate(out_ref[here, here], upper_ref, inverse_ref)
        inverse = inverse_ref[...]

        @pl.loop(lax.div(first, chunk), chunks)
        def _(c):
            rows = pl.ds(pl.multiple_of(c * chunk, chunk), chunk)
            out_ref[rows, here] = dot_t(out_ref[rows, here], inverse)

        out_ref[here, here] = jnp.where(row >= col, upper_ref[...].T, 0.0)

        @pl.loop(0, k)
        def _(i):
            out_ref[pl.ds(pl.multiple_of(i * B, B), B), here] = jnp.zeros((B, B), jnp.float32)

        @pl.loop(k + 1, panels)
        def _(j):
            there = pl.ds(pl.multiple_of(j * B, B), B)
            other = out_ref[there, here]

            @pl.loop(lax.div(j * B, chunk), chunks)
            def _(c):
                rows = pl.ds(pl.multiple_of(c * chunk, chunk), chunk)
                out_ref[rows, there] = out_ref[rows, there] - dot_t(out_ref[rows, here], other)


def factor_columns(pivot, low):
    width = pivot.shape[0]
    total = width + low.shape[0]
    chunk = 2 * B if total % (2 * B) == 0 else B
    return pl.pallas_call(
        functools.partial(factor_kernel, chunk=chunk),
        out_shape=jax.ShapeDtypeStruct((total, width), jnp.float32),
        in_specs=[pl.BlockSpec(memory_space=pltpu.VMEM)] * 2,
        out_specs=pl.BlockSpec(memory_space=pltpu.VMEM),
        scratch_shapes=[pltpu.VMEM((B, B), jnp.float32), pltpu.VMEM((B, B), jnp.float32)],
        compiler_params=pltpu.CompilerParams(vmem_limit_bytes=VMEM_LIMIT),
        cost_estimate=pl.CostEstimate(
            flops=100_000_000_000, bytes_accessed=2 * 4 * total * width, transcendentals=0
        ),
        name="factor_columns",
    )(pivot, low)


def update_kernel(index_ref, valid_ref, low_ref, entries_ref, out_ref):
    count = out_ref.shape[0]
    width = out_ref.shape[2]
    step = 2 * B
    for p in range(count):
        rows = pl.ds(pl.multiple_of(index_ref[p] * B, B), B)
        valid = valid_ref[p]

        @pl.when(valid == 0)
        def _():
            out_ref[p] = jnp.zeros(out_ref.shape[1:], jnp.float32)

        @pl.when(valid != 0)
        def _():
            @pl.loop(0, width // step)
            def _(c):
                cols = pl.ds(pl.multiple_of(c * step, step), step)
                out_ref[p, :, cols] = entries_ref[rows, cols] - dot_t(low_ref[rows, :], low_ref[cols, :])


def placed_update(index, valid, low, entries):
    count = index.shape[0]
    smem = pl.BlockSpec(memory_space=pltpu.SMEM)
    vmem = pl.BlockSpec(memory_space=pltpu.VMEM)
    return pl.pallas_call(
        update_kernel,
        out_shape=jax.ShapeDtypeStruct((count, B, entries.shape[1]), jnp.float32),
        in_specs=[smem, smem, vmem, vmem],
        out_specs=vmem,
        compiler_params=pltpu.CompilerParams(vmem_limit_bytes=VMEM_LIMIT),
        cost_estimate=pl.CostEstimate(
            flops=6 * 2 * count * B * entries.shape[1] * low.shape[1],
            bytes_accessed=4 * 2 * low.size,
            transcendentals=0,
        ),
        name="placed_update",
    )(index, valid, low, entries)


def assemble_kernel(places_ref, flags_ref, base_ref, *refs):
    pieces, out_ref = refs[:-1], refs[-1]
    out_ref[...] = base_ref[...]
    for n, piece in enumerate(pieces):

        @pl.when(flags_ref[n] != 0)
        def _():
            for b in range(piece.shape[2] // B):
                cols = pl.ds(pl.multiple_of(places_ref[n, b] * B, B), B)
                out_ref[:, :, cols] = out_ref[:, :, cols] + piece[:, :, b * B : (b + 1) * B]


def assemble(places, flags, base, pieces):
    smem = pl.BlockSpec(memory_space=pltpu.SMEM)
    vmem = pl.BlockSpec(memory_space=pltpu.VMEM)
    return pl.pallas_call(
        assemble_kernel,
        out_shape=jax.ShapeDtypeStruct(base.shape, jnp.float32),
        in_specs=[smem, smem, vmem] + [vmem] * len(pieces),
        out_specs=vmem,
        compiler_params=pltpu.CompilerParams(vmem_limit_bytes=VMEM_LIMIT),
        cost_estimate=pl.CostEstimate(flops=base.size, bytes_accessed=16 * base.size, transcendentals=0),
        name="assemble",
    )(places, flags, base, *pieces)


def gather_rows(blocks):
    whole = lax.all_gather(blocks[:, None], "rows", axis=1, tiled=True)
    return whole.reshape(-1, blocks.shape[-1])


def own_rows(factor, kept):
    ranks = lax.axis_size("rows")
    width = factor.shape[1]
    top = factor[:width].reshape(kept, ranks, B, width)
    top = lax.dynamic_index_in_dim(top, lax.axis_index("rows"), 1, keepdims=False)
    return jnp.concatenate([top, factor[width:].reshape(kept, B, width)], axis=0)


def on_device(child_front_entries, parent_fronts, parent_of, positions):
    ranks = lax.axis_size("rows")
    rank = lax.axis_index("rows")
    leaf = lax.axis_index("leaf")
    leaves = lax.axis_size("leaf")
    child = child_front_entries[0, :, 0]
    parent = parent_fronts[0, :, 0]
    blocks = child.shape[0]
    kept = PIV // B // ranks

    pivot = gather_rows(child[:kept, :, :PIV])
    entries = gather_rows(child[kept:, :, PIV:])
    low = child[kept:, :, :PIV].reshape(-1, PIV)
    child_factor = factor_columns(pivot, low)
    low_whole = gather_rows(child_factor[PIV:].reshape(kept, B, PIV))

    own = positions[0]
    ids = jnp.arange(blocks, dtype=jnp.int32) * ranks + rank
    match = (ids[:, None] == own[None, :]).astype(jnp.int32)
    valid = jnp.sum(match, axis=1)
    index = jnp.sum(match * jnp.arange(own.shape[0], dtype=jnp.int32)[None, :], axis=1)

    leaf_ids = jnp.arange(leaves, dtype=jnp.int32)
    parent_at = lambda n: jnp.sum(jnp.where(leaf_ids == n, parent_of, 0))
    own_parent = parent_at(leaf)
    is_head = (leaf == 0) | (parent_at(leaf - 1) != own_parent)
    flags = [jnp.int32(1)]
    places = [own]
    for shift in range(1, MOST):
        same = (parent_at(leaf + shift) == own_parent) & (leaf + shift < leaves)
        flags.append(same.astype(jnp.int32))
        places.append(from_behind(own.astype(jnp.float32), "leaf", -shift).astype(jnp.int32))
    flags = jnp.stack(flags)
    places = jnp.stack(places)

    def shifted(update):
        return [update] + [from_behind(update, "leaf", -shift) for shift in range(1, MOST)]

    top_pieces = shifted(placed_update(index[:kept], valid[:kept], low_whole, entries))
    rest_pieces = shifted(placed_update(index[kept:], valid[kept:], low_whole, entries))
    top = assemble(places, flags, parent[:kept], top_pieces)
    parent_pivot = gather_rows(top[:, :, :PIV])
    rest = assemble(places, flags, parent[kept:], rest_pieces)
    parent_factor = factor_columns(parent_pivot, rest[:, :, :PIV].reshape(-1, PIV))
    parent_own = parent_factor[PIV:]
    parent_whole = gather_rows(parent_own.reshape(kept, B, PIV))
    contribution = rest[:, :, PIV:] - dot_t(parent_own, parent_whole).reshape(kept, B, -1)
    return (
        own_rows(child_factor, kept)[None, :, None],
        jnp.where(is_head, own_rows(parent_factor, kept), 0.0)[None, :, None],
        jnp.where(is_head, contribution, 0.0)[None, :, None],
    )


def solution(mesh):
    placed = (
        P("leaf", None, "rows", None, None),
        P("leaf", None, "rows", None, None),
        P(),
        P("leaf", None),
    )
    return jax.shard_map(
        on_device,
        mesh=mesh,
        in_specs=placed,
        out_specs=(
            P("leaf", None, "rows", None, None),
            P("leaf", None, "rows", None, None),
            P("leaf", None, "rows", None, None),
        ),
        check_vma=False,
    )
```

```python
import functools

import jax
import jax.numpy as jnp
from jax import lax
from jax.experimental import pallas as pl
from jax.experimental.pallas import tpu as pltpu
from jax.sharding import PartitionSpec as P

B = 128
PIV = 1024
MOST = 4
SUB = 8
STEP = 4
VMEM_LIMIT = 48 * 1024 * 1024


def from_behind(block, axis, distance):
    devices = range(lax.axis_size(axis))
    route = [(i - distance, i) for i in devices if i - distance in devices]
    return lax.ppermute(block, axis, route)


def dot_t(a, b):
    return lax.dot_general(
        a,
        b,
        (((1,), (1,)), ((), ())),
        precision=lax.Precision.HIGHEST,
        preferred_element_type=jnp.float32,
    )


def eliminate(block, upper_ref, inverse_ref):
    size = block.shape[0]
    groups = size // SUB
    lane = lax.broadcasted_iota(jnp.int32, (SUB, size), 1)
    sub = lax.broadcasted_iota(jnp.int32, (SUB, size), 0)
    left = [block[SUB * u : SUB * (u + 1), :] for u in range(groups)]
    right = [jnp.where(lane == sub + SUB * u, 1.0, 0.0) for u in range(groups)]
    full = lambda x: jnp.broadcast_to(x, (SUB, size))
    for j in range(0, size, STEP):
        t, s = divmod(j, SUB)
        columns = [full(left[t][:, j + i : j + i + 1]) for i in range(STEP)]
        unit_left, unit_right, across = [], [], []
        for i in range(STEP):
            row_left = left[t][s + i : s + i + 1, :]
            row_right = right[t][s + i : s + i + 1, :]
            pivot = columns[i][s + i : s + i + 1, :]
            scale = lax.rsqrt(pivot)
            upper_ref[j + i : j + i + 1, :] = row_left * scale
            inverse_ref[j + i : j + i + 1, :] = row_right * scale
            over = 1.0 / pivot
            unit_left.append(full(row_left * over))
            unit_right.append(full(row_right * over))
            across.append(
                [full(columns[i][s + n : s + n + 1, :] * over) if n > i else None for n in range(STEP)]
            )
            below = jnp.where(sub > s + i, columns[i], 0.0)
            left[t] = left[t] - below * unit_left[i]
            right[t] = right[t] - below * unit_right[i]
            for n in range(i + 1, STEP):
                columns[n] = columns[n] - below * across[i][n]
        for u in range(t + 1, groups):
            columns = [full(left[u][:, j + i : j + i + 1]) for i in range(STEP)]
            for i in range(STEP):
                left[u] = left[u] - columns[i] * unit_left[i]
                right[u] = right[u] - columns[i] * unit_right[i]
                for n in range(i + 1, STEP):
                    columns[n] = columns[n] - columns[i] * across[i][n]


def factor_kernel(*refs, chunk):
    pivot_ref, low_refs = refs[0], refs[1:-4]
    out_ref, inverses_ref, upper_ref, inverse_ref = refs[-4:]
    width = pivot_ref.shape[0]
    total = out_ref.shape[0]
    panels = width // B
    chunks = total // chunk
    out_ref[:width, :] = pivot_ref[...]
    for low_ref in low_refs:
        out_ref[width:, :] = low_ref[...]
    row = lax.broadcasted_iota(jnp.int32, (B, B), 0)
    col = lax.broadcasted_iota(jnp.int32, (B, B), 1)

    @pl.loop(0, panels)
    def _(k):
        first = pl.multiple_of(k * B, B)
        here = pl.ds(first, B)
        eliminate(out_ref[here, here], upper_ref, inverse_ref)
        inverse = inverse_ref[...]
        inverses_ref[here, :] = inverse

        @pl.loop(lax.div(first, chunk), chunks)
        def _(c):
            rows = pl.ds(pl.multiple_of(c * chunk, chunk), chunk)
            out_ref[rows, here] = dot_t(out_ref[rows, here], inverse)

        out_ref[here, here] = jnp.where(row >= col, upper_ref[...].T, 0.0)

        @pl.loop(0, k)
        def _(i):
            out_ref[pl.ds(pl.multiple_of(i * B, B), B), here] = jnp.zeros((B, B), jnp.float32)

        @pl.loop(k + 1, panels)
        def _(j):
            there = pl.ds(pl.multiple_of(j * B, B), B)
            other = out_ref[there, here]

            @pl.loop(lax.div(j * B, chunk), chunks)
            def _(c):
                rows = pl.ds(pl.multiple_of(c * chunk, chunk), chunk)
                out_ref[rows, there] = out_ref[rows, there] - dot_t(out_ref[rows, here], other)


def factor_columns(pivot, *low):
    width = pivot.shape[0]
    total = width + sum(rows.shape[0] for rows in low)
    chunk = 2 * B if total % (2 * B) == 0 else B
    vmem = pl.BlockSpec(memory_space=pltpu.VMEM)
    return pl.pallas_call(
        functools.partial(factor_kernel, chunk=chunk),
        out_shape=(
            jax.ShapeDtypeStruct((total, width), jnp.float32),
            jax.ShapeDtypeStruct((width, B), jnp.float32),
        ),
        in_specs=[vmem] * (1 + len(low)),
        out_specs=(vmem, vmem),
        scratch_shapes=[pltpu.VMEM((B, B), jnp.float32), pltpu.VMEM((B, B), jnp.float32)],
        compiler_params=pltpu.CompilerParams(vmem_limit_bytes=VMEM_LIMIT),
        cost_estimate=pl.CostEstimate(
            flops=100_000_000_000, bytes_accessed=2 * 4 * total * width, transcendentals=0
        ),
        name="factor_columns",
    )(pivot, *low)


def solve_kernel(factor_ref, inverses_ref, low_ref, out_ref):
    for first in range(0, factor_ref.shape[1], B):
        here = slice(first, first + B)
        rest = low_ref[:, here]
        if first > 0:
            rest = rest - dot_t(out_ref[:, :first], factor_ref[here, :first])
        out_ref[:, here] = dot_t(rest, inverses_ref[here, :])


def solve_low(factor, inverses, low):
    vmem = pl.BlockSpec(memory_space=pltpu.VMEM)
    return pl.pallas_call(
        solve_kernel,
        out_shape=jax.ShapeDtypeStruct(low.shape, jnp.float32),
        in_specs=[vmem] * 3,
        out_specs=vmem,
        compiler_params=pltpu.CompilerParams(vmem_limit_bytes=VMEM_LIMIT),
        cost_estimate=pl.CostEstimate(
            flops=6 * low.size * low.shape[1], bytes_accessed=4 * factor.size, transcendentals=0
        ),
        name="solve_low",
    )(factor, inverses, low)


def update_kernel(index_ref, valid_ref, low_ref, entries_ref, out_ref):
    count = out_ref.shape[0]
    width = out_ref.shape[2]
    step = 2 * B
    for p in range(count):
        rows = pl.ds(pl.multiple_of(index_ref[p] * B, B), B)
        valid = valid_ref[p]

        @pl.when(valid == 0)
        def _():
            out_ref[p] = jnp.zeros(out_ref.shape[1:], jnp.float32)

        @pl.when(valid != 0)
        def _():
            @pl.loop(0, width // step)
            def _(c):
                cols = pl.ds(pl.multiple_of(c * step, step), step)
                out_ref[p, :, cols] = entries_ref[rows, cols] - dot_t(low_ref[rows, :], low_ref[cols, :])


def placed_update(index, valid, low, entries):
    count = index.shape[0]
    smem = pl.BlockSpec(memory_space=pltpu.SMEM)
    vmem = pl.BlockSpec(memory_space=pltpu.VMEM)
    return pl.pallas_call(
        update_kernel,
        out_shape=jax.ShapeDtypeStruct((count, B, entries.shape[1]), jnp.float32),
        in_specs=[smem, smem, vmem, vmem],
        out_specs=vmem,
        compiler_params=pltpu.CompilerParams(vmem_limit_bytes=VMEM_LIMIT),
        cost_estimate=pl.CostEstimate(
            flops=6 * 2 * count * B * entries.shape[1] * low.shape[1],
            bytes_accessed=4 * 2 * low.size,
            transcendentals=0,
        ),
        name="placed_update",
    )(index, valid, low, entries)


def assemble_kernel(places_ref, flags_ref, base_ref, *refs):
    pieces, out_ref = refs[:MOST], refs[-1]
    out_ref[...] = base_ref[...]
    for n, piece in enumerate(pieces):

        @pl.when(flags_ref[n] != 0)
        def _():
            for b in range(piece.shape[2] // B):
                cols = pl.ds(pl.multiple_of(places_ref[n, b] * B, B), B)
                out_ref[:, :, cols] = out_ref[:, :, cols] + piece[:, :, b * B : (b + 1) * B]


def assemble(places, flags, base, pieces, *after):
    smem = pl.BlockSpec(memory_space=pltpu.SMEM)
    vmem = pl.BlockSpec(memory_space=pltpu.VMEM)
    return pl.pallas_call(
        assemble_kernel,
        out_shape=jax.ShapeDtypeStruct(base.shape, jnp.float32),
        in_specs=[smem, smem, vmem] + [vmem] * len(pieces) + [pl.BlockSpec(memory_space=pl.ANY)] * len(after),
        out_specs=vmem,
        compiler_params=pltpu.CompilerParams(vmem_limit_bytes=VMEM_LIMIT),
        cost_estimate=pl.CostEstimate(flops=base.size, bytes_accessed=16 * base.size, transcendentals=0),
        name="assemble",
    )(places, flags, base, *pieces, *after)


def gather_rows(blocks):
    whole = lax.all_gather(blocks[:, None], "rows", axis=1, tiled=True)
    return whole.reshape(-1, blocks.shape[-1])


def own_rows(top, low, kept):
    width = top.shape[1]
    top = top.reshape(kept, -1, B, width)
    top = lax.dynamic_index_in_dim(top, lax.axis_index("rows"), 1, keepdims=False)
    return jnp.concatenate([top, low.reshape(kept, B, width)], axis=0)


def on_device(child_front_entries, parent_fronts, parent_of, positions):
    ranks = lax.axis_size("rows")
    rank = lax.axis_index("rows")
    leaf = lax.axis_index("leaf")
    leaves = lax.axis_size("leaf")
    child = child_front_entries[0, :, 0]
    parent = parent_fronts[0, :, 0]
    blocks = child.shape[0]
    kept = PIV // B // ranks

    pivot = gather_rows(child[:kept, :, :PIV])
    entries = gather_rows(child[kept:, :, PIV:])
    low = child[kept:, :, :PIV].reshape(-1, PIV)
    child_factor, _ = factor_columns(pivot, low)
    low_whole = gather_rows(child_factor[PIV:].reshape(kept, B, PIV))

    own = positions[0]
    ids = jnp.arange(blocks, dtype=jnp.int32) * ranks + rank
    match = (ids[:, None] == own[None, :]).astype(jnp.int32)
    valid = jnp.sum(match, axis=1)
    index = jnp.sum(match * jnp.arange(own.shape[0], dtype=jnp.int32)[None, :], axis=1)

    leaf_ids = jnp.arange(leaves, dtype=jnp.int32)
    parent_at = lambda n: jnp.sum(jnp.where(leaf_ids == n, parent_of, 0))
    own_parent = parent_at(leaf)
    is_head = (leaf == 0) | (parent_at(leaf - 1) != own_parent)
    flags = [jnp.int32(1)]
    places = [own]
    for shift in range(1, MOST):
        same = (parent_at(leaf + shift) == own_parent) & (leaf + shift < leaves)
        flags.append(same.astype(jnp.int32))
        places.append(from_behind(own.astype(jnp.float32), "leaf", -shift).astype(jnp.int32))
    flags = jnp.stack(flags)
    places = jnp.stack(places)

    def shifted(update):
        return [update] + [from_behind(update, "leaf", -shift) for shift in range(1, MOST)]

    top_pieces = shifted(placed_update(index[:kept], valid[:kept], low_whole, entries))
    rest_pieces = shifted(placed_update(index[kept:], valid[kept:], low_whole, entries))
    top = assemble(places, flags, parent[:kept], top_pieces)
    parent_pivot = gather_rows(top[:, :, :PIV])
    parent_top, inverses = factor_columns(parent_pivot)
    rest = assemble(places, flags, parent[kept:], rest_pieces, inverses)
    parent_own = solve_low(parent_top, inverses, rest[:, :, :PIV].reshape(-1, PIV))
    parent_whole = gather_rows(parent_own.reshape(kept, B, PIV))
    contribution = rest[:, :, PIV:] - dot_t(parent_own, parent_whole).reshape(kept, B, -1)
    return (
        own_rows(child_factor[:PIV], child_factor[PIV:], kept)[None, :, None],
        jnp.where(is_head, own_rows(parent_top, parent_own, kept), 0.0)[None, :, None],
        jnp.where(is_head, contribution, 0.0)[None, :, None],
    )


def solution(mesh):
    placed = (
        P("leaf", None, "rows", None, None),
        P("leaf", None, "rows", None, None),
        P(),
        P("leaf", None),
    )
    return jax.shard_map(
        on_device,
        mesh=mesh,
        in_specs=placed,
        out_specs=(
            P("leaf", None, "rows", None, None),
            P("leaf", None, "rows", None, None),
            P("leaf", None, "rows", None, None),
        ),
        check_vma=False,
    )
```

```python
import functools

import jax
import jax.numpy as jnp
from jax import lax
from jax.experimental import pallas as pl
from jax.experimental.pallas import tpu as pltpu
from jax.sharding import PartitionSpec as P

B = 128
PIV = 1024
MOST = 4
SUB = 8
STEP = 8
VMEM_LIMIT = 48 * 1024 * 1024


def from_behind(block, axis, distance):
    devices = range(lax.axis_size(axis))
    route = [(i - distance, i) for i in devices if i - distance in devices]
    return lax.ppermute(block, axis, route)


def dot_t(a, b):
    return lax.dot_general(
        a,
        b,
        (((1,), (1,)), ((), ())),
        precision=lax.Precision.HIGHEST,
        preferred_element_type=jnp.float32,
    )


def eliminate(block, upper_ref, inverse_ref):
    size = block.shape[0]
    groups = size // SUB
    lane = lax.broadcasted_iota(jnp.int32, (SUB, size), 1)
    sub = lax.broadcasted_iota(jnp.int32, (SUB, size), 0)
    left = [block[SUB * u : SUB * (u + 1), :] for u in range(groups)]
    right = [jnp.where(lane == sub + SUB * u, 1.0, 0.0) for u in range(groups)]
    full = lambda x: jnp.broadcast_to(x, (SUB, size))
    for j in range(0, size, STEP):
        t, s = divmod(j, SUB)
        columns = [full(left[t][:, j + i : j + i + 1]) for i in range(STEP)]
        unit_left, unit_right, across = [], [], []
        for i in range(STEP):
            row_left = left[t][s + i : s + i + 1, :]
            row_right = right[t][s + i : s + i + 1, :]
            pivot = columns[i][s + i : s + i + 1, :]
            scale = lax.rsqrt(pivot)
            upper_ref[j + i : j + i + 1, :] = row_left * scale
            inverse_ref[j + i : j + i + 1, :] = row_right * scale
            over = 1.0 / pivot
            unit_left.append(full(row_left * over))
            unit_right.append(full(row_right * over))
            across.append(
                [full(columns[i][s + n : s + n + 1, :] * over) if n > i else None for n in range(STEP)]
            )
            below = jnp.where(sub > s + i, columns[i], 0.0)
            left[t] = left[t] - below * unit_left[i]
            right[t] = right[t] - below * unit_right[i]
            for n in range(i + 1, STEP):
                columns[n] = columns[n] - below * across[i][n]
        for u in range(t + 1, groups):
            columns = [full(left[u][:, j + i : j + i + 1]) for i in range(STEP)]
            for i in range(STEP):
                left[u] = left[u] - columns[i] * unit_left[i]
                right[u] = right[u] - columns[i] * unit_right[i]
                for n in range(i + 1, STEP):
                    columns[n] = columns[n] - columns[i] * across[i][n]


def factor_kernel(*refs, chunk):
    pivot_ref, low_refs = refs[0], refs[1:-4]
    out_ref, inverses_ref, upper_ref, inverse_ref = refs[-4:]
    width = pivot_ref.shape[0]
    total = out_ref.shape[0]
    panels = width // B
    chunks = total // chunk
    out_ref[:width, :] = pivot_ref[...]
    for low_ref in low_refs:
        out_ref[width:, :] = low_ref[...]
    row = lax.broadcasted_iota(jnp.int32, (B, B), 0)
    col = lax.broadcasted_iota(jnp.int32, (B, B), 1)

    @pl.loop(0, panels)
    def _(k):
        first = pl.multiple_of(k * B, B)
        here = pl.ds(first, B)
        eliminate(out_ref[here, here], upper_ref, inverse_ref)
        inverse = inverse_ref[...]
        inverses_ref[here, :] = inverse

        @pl.loop(lax.div(first, chunk), chunks)
        def _(c):
            rows = pl.ds(pl.multiple_of(c * chunk, chunk), chunk)
            out_ref[rows, here] = dot_t(out_ref[rows, here], inverse)

        out_ref[here, here] = jnp.where(row >= col, upper_ref[...].T, 0.0)

        @pl.loop(0, k)
        def _(i):
            out_ref[pl.ds(pl.multiple_of(i * B, B), B), here] = jnp.zeros((B, B), jnp.float32)

        @pl.loop(k + 1, panels)
        def _(j):
            there = pl.ds(pl.multiple_of(j * B, B), B)
            other = out_ref[there, here]

            @pl.loop(lax.div(j * B, chunk), chunks)
            def _(c):
                rows = pl.ds(pl.multiple_of(c * chunk, chunk), chunk)
                out_ref[rows, there] = out_ref[rows, there] - dot_t(out_ref[rows, here], other)


def factor_columns(pivot, *low):
    width = pivot.shape[0]
    total = width + sum(rows.shape[0] for rows in low)
    chunk = 2 * B if total % (2 * B) == 0 else B
    vmem = pl.BlockSpec(memory_space=pltpu.VMEM)
    return pl.pallas_call(
        functools.partial(factor_kernel, chunk=chunk),
        out_shape=(
            jax.ShapeDtypeStruct((total, width), jnp.float32),
            jax.ShapeDtypeStruct((width, B), jnp.float32),
        ),
        in_specs=[vmem] * (1 + len(low)),
        out_specs=(vmem, vmem),
        scratch_shapes=[pltpu.VMEM((B, B), jnp.float32), pltpu.VMEM((B, B), jnp.float32)],
        compiler_params=pltpu.CompilerParams(vmem_limit_bytes=VMEM_LIMIT),
        cost_estimate=pl.CostEstimate(
            flops=100_000_000_000, bytes_accessed=2 * 4 * total * width, transcendentals=0
        ),
        name="factor_columns",
    )(pivot, *low)


def solve_kernel(factor_ref, inverses_ref, low_ref, out_ref):
    for first in range(0, factor_ref.shape[1], B):
        here = slice(first, first + B)
        rest = low_ref[:, here]
        if first > 0:
            rest = rest - dot_t(out_ref[:, :first], factor_ref[here, :first])
        out_ref[:, here] = dot_t(rest, inverses_ref[here, :])


def solve_low(factor, inverses, low):
    vmem = pl.BlockSpec(memory_space=pltpu.VMEM)
    return pl.pallas_call(
        solve_kernel,
        out_shape=jax.ShapeDtypeStruct(low.shape, jnp.float32),
        in_specs=[vmem] * 3,
        out_specs=vmem,
        compiler_params=pltpu.CompilerParams(vmem_limit_bytes=VMEM_LIMIT),
        cost_estimate=pl.CostEstimate(
            flops=6 * low.size * low.shape[1], bytes_accessed=4 * factor.size, transcendentals=0
        ),
        name="solve_low",
    )(factor, inverses, low)


def update_kernel(index_ref, valid_ref, low_ref, entries_ref, out_ref):
    count = out_ref.shape[0]
    width = out_ref.shape[2]
    step = 2 * B
    for p in range(count):
        rows = pl.ds(pl.multiple_of(index_ref[p] * B, B), B)
        valid = valid_ref[p]

        @pl.when(valid == 0)
        def _():
            out_ref[p] = jnp.zeros(out_ref.shape[1:], jnp.float32)

        @pl.when(valid != 0)
        def _():
            @pl.loop(0, width // step)
            def _(c):
                cols = pl.ds(pl.multiple_of(c * step, step), step)
                out_ref[p, :, cols] = entries_ref[rows, cols] - dot_t(low_ref[rows, :], low_ref[cols, :])


def placed_update(index, valid, low, entries):
    count = index.shape[0]
    smem = pl.BlockSpec(memory_space=pltpu.SMEM)
    vmem = pl.BlockSpec(memory_space=pltpu.VMEM)
    return pl.pallas_call(
        update_kernel,
        out_shape=jax.ShapeDtypeStruct((count, B, entries.shape[1]), jnp.float32),
        in_specs=[smem, smem, vmem, vmem],
        out_specs=vmem,
        compiler_params=pltpu.CompilerParams(vmem_limit_bytes=VMEM_LIMIT),
        cost_estimate=pl.CostEstimate(
            flops=6 * 2 * count * B * entries.shape[1] * low.shape[1],
            bytes_accessed=4 * 2 * low.size,
            transcendentals=0,
        ),
        name="placed_update",
    )(index, valid, low, entries)


def assemble_kernel(places_ref, flags_ref, base_ref, *refs):
    pieces, out_ref = refs[:MOST], refs[-1]
    out_ref[...] = base_ref[...]
    for n, piece in enumerate(pieces):

        @pl.when(flags_ref[n] != 0)
        def _():
            for b in range(piece.shape[2] // B):
                cols = pl.ds(pl.multiple_of(places_ref[n, b] * B, B), B)
                out_ref[:, :, cols] = out_ref[:, :, cols] + piece[:, :, b * B : (b + 1) * B]


def assemble(places, flags, base, pieces, *after):
    smem = pl.BlockSpec(memory_space=pltpu.SMEM)
    vmem = pl.BlockSpec(memory_space=pltpu.VMEM)
    return pl.pallas_call(
        assemble_kernel,
        out_shape=jax.ShapeDtypeStruct(base.shape, jnp.float32),
        in_specs=[smem, smem, vmem] + [vmem] * len(pieces) + [pl.BlockSpec(memory_space=pl.ANY)] * len(after),
        out_specs=vmem,
        compiler_params=pltpu.CompilerParams(vmem_limit_bytes=VMEM_LIMIT),
        cost_estimate=pl.CostEstimate(flops=base.size, bytes_accessed=16 * base.size, transcendentals=0),
        name="assemble",
    )(places, flags, base, *pieces, *after)


def gather_rows(blocks):
    whole = lax.all_gather(blocks[:, None], "rows", axis=1, tiled=True)
    return whole.reshape(-1, blocks.shape[-1])


def own_rows(top, low, kept):
    width = top.shape[1]
    top = top.reshape(kept, -1, B, width)
    top = lax.dynamic_index_in_dim(top, lax.axis_index("rows"), 1, keepdims=False)
    return jnp.concatenate([top, low.reshape(kept, B, width)], axis=0)


def on_device(child_front_entries, parent_fronts, parent_of, positions):
    ranks = lax.axis_size("rows")
    rank = lax.axis_index("rows")
    leaf = lax.axis_index("leaf")
    leaves = lax.axis_size("leaf")
    child = child_front_entries[0, :, 0]
    parent = parent_fronts[0, :, 0]
    blocks = child.shape[0]
    kept = PIV // B // ranks

    pivot = gather_rows(child[:kept, :, :PIV])
    entries = gather_rows(child[kept:, :, PIV:])
    low = child[kept:, :, :PIV].reshape(-1, PIV)
    child_factor, _ = factor_columns(pivot, low)
    low_whole = gather_rows(child_factor[PIV:].reshape(kept, B, PIV))

    own = positions[0]
    ids = jnp.arange(blocks, dtype=jnp.int32) * ranks + rank
    match = (ids[:, None] == own[None, :]).astype(jnp.int32)
    valid = jnp.sum(match, axis=1)
    index = jnp.sum(match * jnp.arange(own.shape[0], dtype=jnp.int32)[None, :], axis=1)

    leaf_ids = jnp.arange(leaves, dtype=jnp.int32)
    parent_at = lambda n: jnp.sum(jnp.where(leaf_ids == n, parent_of, 0))
    own_parent = parent_at(leaf)
    is_head = (leaf == 0) | (parent_at(leaf - 1) != own_parent)
    flags = [jnp.int32(1)]
    places = [own]
    for shift in range(1, MOST):
        same = (parent_at(leaf + shift) == own_parent) & (leaf + shift < leaves)
        flags.append(same.astype(jnp.int32))
        places.append(from_behind(own.astype(jnp.float32), "leaf", -shift).astype(jnp.int32))
    flags = jnp.stack(flags)
    places = jnp.stack(places)

    def shifted(update):
        return [update] + [from_behind(update, "leaf", -shift) for shift in range(1, MOST)]

    top_pieces = shifted(placed_update(index[:kept], valid[:kept], low_whole, entries))
    rest_pieces = shifted(placed_update(index[kept:], valid[kept:], low_whole, entries))
    top = assemble(places, flags, parent[:kept], top_pieces)
    parent_pivot = gather_rows(top[:, :, :PIV])
    parent_top, inverses = factor_columns(parent_pivot)
    rest = assemble(places, flags, parent[kept:], rest_pieces, inverses)
    parent_own = solve_low(parent_top, inverses, rest[:, :, :PIV].reshape(-1, PIV))
    parent_whole = gather_rows(parent_own.reshape(kept, B, PIV))
    contribution = rest[:, :, PIV:] - dot_t(parent_own, parent_whole).reshape(kept, B, -1)
    return (
        own_rows(child_factor[:PIV], child_factor[PIV:], kept)[None, :, None],
        jnp.where(is_head, own_rows(parent_top, parent_own, kept), 0.0)[None, :, None],
        jnp.where(is_head, contribution, 0.0)[None, :, None],
    )


def solution(mesh):
    placed = (
        P("leaf", None, "rows", None, None),
        P("leaf", None, "rows", None, None),
        P(),
        P("leaf", None),
    )
    return jax.shard_map(
        on_device,
        mesh=mesh,
        in_specs=placed,
        out_specs=(
            P("leaf", None, "rows", None, None),
            P("leaf", None, "rows", None, None),
            P("leaf", None, "rows", None, None),
        ),
        check_vma=False,
    )
```
